32 devices in a mesh: groups: 2 (over x), dp: 2 (over core), tensor: 8 (over z, y).
Axes of the slice: x: 2, y: 2, z: 4, core: 2. Of those that a mesh axis runs over, the one named last changes fastest.
Arguments:
- tokens: bfloat16 [512, 4608], P(('groups', 'dp', 'tensor')), parts along dimension 0, may hold values from -6 to 6
- gate_weight: bfloat16 [3584, 4608], P('tensor'), may hold values from -0.09375 to 0.09375
- up_weight: bfloat16 [3584, 4608], P('tensor'), may hold values from -0.09375 to 0.09375
- down_weight: bfloat16 [3584, 4608], P('tensor'), may hold values from -0.09375 to 0.09375
- format_codes: int32 [3, 3584], P(None, 'tensor'), may hold values from 0 to 1
- scale_exponents: int32 [3, 3584], P(None, 'tensor'), may hold values from 6 to 16, as said below
Outputs:
- mixed: bfloat16 [512, 4608], P(('groups', 'dp', 'tensor')), parts along dimension 0
The draws below stay inside these ranges and needn't reach their ends.
There are 2 independent parts, one for each index of `groups`. The reference program is written for one: setup_inputs(seed, part) draws one part's arguments, and reference() takes and returns one part's arrays. A program takes and returns all parts, laid end to end along the dimension named above; an argument that names none is the same for every part. Nothing has to cross between parts.
Inputs may be any that keep to these rules, and one draw needn't show every extreme that they name: `scale_exponents`: each exponent minus (7 + 8 times its format code) is -1, 0 or 1.
All inputs are finite; a program needn't handle non-finite values.
Results may differ from the reference program's by a relative error of at most 0.0049.
Values may be sent and summed in bfloat16 or wider, within the bound.
A program may use at most 128 MiB of HBM per device.

```python
import jax
import jax.numpy as jnp
from jax import lax

D = 4608
FFN = 3584
TOKENS = 256


def shared_codes(key):
    codes = jax.random.randint(jax.random.fold_in(key, 11), (3, FFN), 0, 2).astype(jnp.int32)
    codes = codes.at[0, 0].set(0)
    codes = codes.at[0, 1].set(1)
    return codes


def draw_format_codes(key, part):
    codes = shared_codes(key)
    return codes


def draw_scale_exponents(key, part):
    codes = shared_codes(key)
    key = jax.random.fold_in(key, 2)
    offset = jax.random.randint(key, (3, FFN), -1, 2).astype(jnp.int32)
    offset = offset.at[0, 0].set(-1)
    offset = offset.at[0, 1].set(1)
    return (7 + 8 * codes + offset).astype(jnp.int32)


def shard_levels(stream_key, extent, pieces, low, largest):
    gain, own = 1.0, jax.random.fold_in(stream_key, 6)
    for position, shards_of in pieces:
        steps = jnp.exp(jax.random.uniform(jax.random.fold_in(own, position), (shards_of,), jnp.float32, low / len(pieces), largest / len(pieces)))
        gain = gain * jnp.repeat(steps, extent[position] // shards_of).reshape([-1 if axis == position else 1 for axis in range(len(extent))])
    return gain


def centred(key, dims, width, most, shards=(), dtype=jnp.bfloat16):
    array = jax.random.normal(key, dims, jnp.float32) * width
    if len(shards) > 0:
        array = shard_levels(key, dims, shards, -0.22, 0.18) * array
    return jnp.clip(array, min=-most, max=most).astype(dtype)


def setup_inputs(seed: int = 0, part: int = 0) -> dict:
    seeds = jax.random.split(jax.random.key(seed), 7)
    part_splits = jax.random.split(jax.random.fold_in(seeds[6], part), 7)
    tokens = centred(part_splits[0], (TOKENS, D), 1.0, 6.0, ((0, 16),))
    gate_weight = centred(seeds[1], (FFN, D), D ** -0.5, 0.09375, ((0, 8),))
    up_weight = centred(seeds[2], (FFN, D), D ** -0.5, 0.09375, ((0, 8),))
    down_weight = centred(seeds[3], (FFN, D), FFN ** -0.5, 0.09375, ((0, 8),))
    format_codes = draw_format_codes(jax.random.fold_in(seeds[6], 71), part)
    scale_exponents = draw_scale_exponents(jax.random.fold_in(seeds[6], 71), part)
    return {"tokens": tokens, "gate_weight": gate_weight, "up_weight": up_weight, "down_weight": down_weight, "format_codes": format_codes, "scale_exponents": scale_exponents}


def dequant_factors(format_codes, scale_exponents):
    offset = scale_exponents - (7 + 8 * format_codes)
    return jnp.exp2(offset.astype(jnp.float32))


def project_rows(rows, weight):
    return lax.dot_general(rows, weight, (((1,), (1,)), ((), ())), preferred_element_type=jnp.float32)


def reference(tokens, gate_weight, up_weight, down_weight, format_codes, scale_exponents):
    factor = dequant_factors(format_codes, scale_exponents)
    gate = project_rows(tokens, gate_weight) * factor[0][None, :]
    up_part = project_rows(tokens, up_weight) * factor[1][None, :]
    hidden = (jax.nn.gelu(gate, approximate=True) * up_part).astype(jnp.bfloat16)
    scaled_down = (down_weight.astype(jnp.float32) * factor[2][:, None]).astype(jnp.bfloat16)
    mixed = jnp.dot(hidden, scaled_down, preferred_element_type=jnp.float32)
    return mixed.astype(jnp.bfloat16)
```

```python
import functools
import math

import jax
import jax.numpy as jnp
from jax import lax
from jax.experimental import pallas as pl
from jax.experimental.pallas import tpu as pltpu
from jax.sharding import PartitionSpec as P

MESH = pl.DeviceIdType.MESH
F32 = jnp.float32
BF16 = jnp.bfloat16


def lines_of(n):
    inner = math.isqrt(n)
    while n % inner:
        inner -= 1
    return n // inner, inner


def kernel(
    A, B, tokens, gate_w, up_w, down_w, codes, exps, out,
    tok, wg, wu, wd, hid, part, own, sbuf, ybuf, rbuf, lbuf,
    w_sem, ag_recv, ag_r, ag_l, ag_y, y_send, y_recv, c_send, r_recv, l_recv,
):
    me = lax.axis_index("tensor")
    a, b = me // B, lax.rem(me, B)
    rows, D = tokens.shape
    has_left, has_right = a > 0, a < A - 1

    def dev(za, yb):
        return {"tensor": za * B + yb}

    def rcopy(src, dst, ssem, rsem, device):
        return pltpu.make_async_remote_copy(
            src_ref=src, dst_ref=dst, send_sem=ssem, recv_sem=rsem,
            device_id=device, device_id_type=MESH,
        )

    loads = [
        pltpu.make_async_copy(src, dst, w_sem.at[i])
        for i, (src, dst) in enumerate(((gate_w, wg), (up_w, wu), (down_w, wd)))
    ]
    for load in loads:
        load.start()

    barrier = pltpu.get_barrier_semaphore()
    partners = [lax.rem(b + o, B) for o in range(1, B)]
    for p in partners:
        pl.semaphore_signal(barrier, inc=1, device_id=dev(a, p), device_id_type=MESH)

    @pl.when(has_left)
    def _():
        pl.semaphore_signal(barrier, inc=1, device_id=dev(a - 1, b), device_id_type=MESH)

    @pl.when(has_right)
    def _():
        pl.semaphore_signal(barrier, inc=1, device_id=dev(a + 1, b), device_id_type=MESH)

    peers = B - 1 + jnp.minimum(a, 1) + jnp.minimum(A - 1 - a, 1)
    pl.semaphore_wait(barrier, peers)

    def ag_right(t, src):
        return rcopy(src, tok.at[b, t], ag_r.at[t], ag_recv.at[b, t], dev(a + 1, b))

    def ag_left(t, src):
        return rcopy(src, tok.at[b, t], ag_l.at[t], ag_recv.at[b, t], dev(a - 1, b))

    def ag_across(t, o, src):
        return rcopy(src, tok.at[b, t], ag_y.at[o - 1, t], ag_recv.at[b, t], dev(a, partners[o - 1]))

    def ag_wait(line, t):
        rcopy(tok.at[line, t], tok.at[line, t], ag_r.at[t], ag_recv.at[line, t], dev(a, partners[0])).wait_recv()

    @pl.when(has_right)
    def _():
        ag_right(a, tokens).start()

    @pl.when(has_left)
    def _():
        ag_left(a, tokens).start()

    for o in range(1, B):
        ag_across(a, o, tokens).start()
    tok[b, a] = tokens[...]

    for s in range(1, A):
        t_left, t_right = a - s, a + s

        @pl.when(t_left >= 0)
        def _():
            ag_wait(b, t_left)

            @pl.when(has_right)
            def _():
                ag_right(t_left, tok.at[b, t_left]).start()

            for o in range(1, B):
                ag_across(t_left, o, tok.at[b, t_left]).start()

        @pl.when(t_right < A)
        def _():
            ag_wait(b, t_right)

            @pl.when(has_left)
            def _():
                ag_left(t_right, tok.at[b, t_right]).start()

            for o in range(1, B):
                ag_across(t_right, o, tok.at[b, t_right]).start()

    offset = exps[...] - (7 + 8 * codes[...])
    factor = jnp.where(offset < 0, 0.5, jnp.where(offset > 0, 2.0, 1.0)).astype(F32)

    def project(line):
        x = tok[line].reshape(A * rows, D)
        dims = (((1,), (1,)), ((), ()))
        gate = lax.dot_general(x, wg[...], dims, preferred_element_type=F32) * factor[0:1, :]
        up = lax.dot_general(x, wu[...], dims, preferred_element_type=F32) * factor[1:2, :]
        h = (jax.nn.gelu(gate, approximate=True) * up).astype(BF16)
        hid[line] = (h.astype(F32) * factor[2:3, :]).astype(BF16)

    loads[0].wait()
    loads[1].wait()
    project(b)
    loads[2].wait()

    def y_copy(t, o):
        return rcopy(
            part.at[partners[o - 1], t], ybuf.at[o - 1, t],
            y_send.at[o - 1, t], y_recv.at[o - 1, t], dev(a, partners[o - 1]),
        )

    def by_distance(body):
        for d in range(A - 1, 0, -1):
            for t in (a + d, a - d):
                @pl.when((t >= 0) & (t < A))
                def _():
                    body(t)
        body(a)

    for o in range(1, B):
        line = partners[o - 1]
        for t in range(A):
            ag_wait(line, t)
        project(line)
        y = jnp.dot(hid[line], wd[...], preferred_element_type=F32)
        part[line] = y.astype(BF16).reshape(A, rows, D)
        by_distance(lambda t: y_copy(t, o).start())

    own[...] = jnp.dot(hid[b], wd[...], preferred_element_type=F32).reshape(A, rows, D)

    def right_copy(t):
        return rcopy(sbuf.at[t], rbuf.at[t], c_send.at[t], r_recv.at[t], dev(a + 1, b))

    def left_copy(t):
        return rcopy(sbuf.at[t], lbuf.at[t], c_send.at[t], l_recv.at[t], dev(a - 1, b))

    def gather_y(t):
        total = own[t]
        for o in range(1, B):
            y_copy(t, o).wait_recv()
            total += ybuf[o - 1, t].astype(F32)
        return total

    for d in range(A - 1, 0, -1):
        for right in (True, False):
            t = a + d if right else a - d

            @pl.when((t < A) if right else (t >= 0))
            def _():
                own[t] = gather_y(t)

                @pl.when(has_left if right else has_right)
                def _():
                    if right:
                        right_copy(t).wait_recv()
                        own[t] += rbuf[t].astype(F32)
                    else:
                        left_copy(t).wait_recv()
                        own[t] += lbuf[t].astype(F32)

                sbuf[t] = own[t].astype(BF16)
                (right_copy(t) if right else left_copy(t)).start()

    own[a] = gather_y(a)

    @pl.when(has_left)
    def _():
        right_copy(a).wait_recv()
        own[a] += rbuf[a].astype(F32)

    @pl.when(has_right)
    def _():
        left_copy(a).wait_recv()
        own[a] += lbuf[a].astype(F32)

    out[...] = own[a].astype(out.dtype)

    for t in range(A):
        @pl.when(has_right & (t <= a))
        def _():
            ag_right(t, tokens).wait_send()

        @pl.when(has_left & (t >= a))
        def _():
            ag_left(t, tokens).wait_send()

        for o in range(1, B):
            ag_across(t, o, tokens).wait_send()
            y_copy(t, o).wait_send()

        @pl.when(t != a)
        def _():
            right_copy(t).wait_send()


def on_device(n, tokens, gate_weight, up_weight, down_weight, format_codes, scale_exponents):
    A, B = lines_of(n)
    rows, D = tokens.shape
    hidden = gate_weight.shape[0]
    vmem = pl.BlockSpec(memory_space=pltpu.VMEM)
    hbm = pl.BlockSpec(memory_space=pl.ANY)
    dma = pltpu.SemaphoreType.DMA
    return pl.pallas_call(
        functools.partial(kernel, A, B),
        out_shape=jax.ShapeDtypeStruct((rows, D), BF16),
        in_specs=[vmem, hbm, hbm, hbm, vmem, vmem],
        out_specs=vmem,
        scratch_shapes=[
            pltpu.VMEM((B, A, rows, D), BF16),
            pltpu.VMEM((hidden, D), BF16),
            pltpu.VMEM((hidden, D), BF16),
            pltpu.VMEM((hidden, D), BF16),
            pltpu.VMEM((B, A * rows, hidden), BF16),
            pltpu.VMEM((B, A, rows, D), BF16),
            pltpu.VMEM((A, rows, D), F32),
            pltpu.VMEM((A, rows, D), BF16),
            pltpu.VMEM((B - 1, A, rows, D), BF16),
            pltpu.VMEM((A, rows, D), BF16),
            pltpu.VMEM((A, rows, D), BF16),
            dma((3,)),
            dma((B, A)),
            dma((A,)),
            dma((A,)),
            dma((B - 1, A)),
            dma((B - 1, A)),
            dma((B - 1, A)),
            dma((A,)),
            dma((A,)),
            dma((A,)),
        ],
        compiler_params=pltpu.CompilerParams(
            collective_id=0, has_side_effects=True, vmem_limit_bytes=60 * 2**20
        ),
    )(tokens, gate_weight, up_weight, down_weight, format_codes, scale_exponents)


def solution(mesh):
    return jax.shard_map(
        functools.partial(on_device, mesh.shape["tensor"]),
        mesh=mesh,
        in_specs=(
            P(("groups", "dp", "tensor"), None),
            P("tensor", None),
            P("tensor", None),
            P("tensor", None),
            P(None, "tensor"),
            P(None, "tensor"),
        ),
        out_specs=P(("groups", "dp", "tensor"), None),
        check_vma=False,
    )
```

```python
import functools
import math

import jax
import jax.numpy as jnp
from jax import lax
from jax.experimental import pallas as pl
from jax.experimental.pallas import tpu as pltpu
from jax.sharding import PartitionSpec as P

MESH = pl.DeviceIdType.MESH
F32 = jnp.float32
BF16 = jnp.bfloat16


def lines_of(n):
    inner = math.isqrt(n)
    while n % inner:
        inner -= 1
    return n // inner, inner


def kernel(
    A, B, C, tokens, gate_w, up_w, down_w, codes_in, exps_in, out,
    tok, wg, wu, wd, codes, exps, hid, part, own, sbuf, ybuf, rbuf, lbuf,
    w_sem, tok_sem, ag_recv, ag_r, ag_l, ag_y, y_send, y_recv, c_send, r_recv, l_recv,
):
    me = lax.axis_index("tensor")
    a, b = me // B, lax.rem(me, B)
    rows, D = tokens.shape
    width = D // C
    has_left, has_right = a > 0, a < A - 1

    def cols(c):
        return pl.ds(c * width, width)

    def dev(za, yb):
        return {"tensor": za * B + yb}

    def rcopy(src, dst, ssem, rsem, device):
        return pltpu.make_async_remote_copy(
            src_ref=src, dst_ref=dst, send_sem=ssem, recv_sem=rsem,
            device_id=device, device_id_type=MESH,
        )

    barrier = pltpu.get_barrier_semaphore()
    partners = [lax.rem(b + o, B) for o in range(1, B)]
    for p in partners:
        pl.semaphore_signal(barrier, inc=1, device_id=dev(a, p), device_id_type=MESH)

    @pl.when(has_left)
    def _():
        pl.semaphore_signal(barrier, inc=1, device_id=dev(a - 1, b), device_id_type=MESH)

    @pl.when(has_right)
    def _():
        pl.semaphore_signal(barrier, inc=1, device_id=dev(a + 1, b), device_id_type=MESH)

    own_tokens = pltpu.make_async_copy(tokens, tok.at[b, a], tok_sem)
    own_tokens.start()
    loads = [
        pltpu.make_async_copy(src, dst, w_sem.at[i])
        for i, (src, dst) in enumerate(
            ((codes_in, codes), (exps_in, exps), (gate_w, wg), (up_w, wu), (down_w, wd))
        )
    ]
    for load in loads:
        load.start()

    peers = B - 1 + jnp.minimum(a, 1) + jnp.minimum(A - 1 - a, 1)
    pl.semaphore_wait(barrier, peers)

    def ag_copy(t, c, src, ssem, device):
        return rcopy(
            src.at[:, cols(c)], tok.at[b, t, :, cols(c)], ssem, ag_recv.at[b, t, c], device
        )

    def ag_right(t, c, src):
        return ag_copy(t, c, src, ag_r.at[t, c], dev(a + 1, b))

    def ag_left(t, c, src):
        return ag_copy(t, c, src, ag_l.at[t, c], dev(a - 1, b))

    def ag_across(t, c, o, src):
        return ag_copy(t, c, src, ag_y.at[o - 1, t, c], dev(a, partners[o - 1]))

    def ag_wait(line, t, c):
        block = tok.at[line, t, :, cols(c)]
        rcopy(block, block, ag_r.at[t, c], ag_recv.at[line, t, c], dev(a, partners[0])).wait_recv()

    for c in range(C):
        @pl.when(has_right)
        def _():
            ag_right(a, c, tokens).start()

        @pl.when(has_left)
        def _():
            ag_left(a, c, tokens).start()

        for o in range(1, B):
            ag_across(a, c, o, tokens).start()

    for s in range(1, A):
        t_left, t_right = a - s, a + s
        for c in range(C):
            @pl.when(t_left >= 0)
            def _():
                ag_wait(b, t_left, c)

                @pl.when(has_right)
                def _():
                    ag_right(t_left, c, tok.at[b, t_left]).start()

                for o in range(1, B):
                    ag_across(t_left, c, o, tok.at[b, t_left]).start()

            @pl.when(t_right < A)
            def _():
                ag_wait(b, t_right, c)

                @pl.when(has_left)
                def _():
                    ag_left(t_right, c, tok.at[b, t_right]).start()

                for o in range(1, B):
                    ag_across(t_right, c, o, tok.at[b, t_right]).start()

    loads[0].wait()
    loads[1].wait()
    offset = exps[...] - (7 + 8 * codes[...])
    factor = jnp.where(offset < 0, 0.5, jnp.where(offset > 0, 2.0, 1.0)).astype(F32)

    def project(line):
        x = tok[line].reshape(A * rows, D)
        dims = (((1,), (1,)), ((), ()))
        gate = lax.dot_general(x, wg[...], dims, preferred_element_type=F32) * factor[0:1, :]
        up = lax.dot_general(x, wu[...], dims, preferred_element_type=F32) * factor[1:2, :]
        h = (jax.nn.gelu(gate, approximate=True) * up).astype(BF16)
        hid[line] = (h.astype(F32) * factor[2:3, :]).astype(BF16)

    own_tokens.wait()
    loads[2].wait()
    loads[3].wait()
    project(b)
    loads[4].wait()

    def y_copy(t, c, o):
        return rcopy(
            part.at[partners[o - 1], t, :, cols(c)], ybuf.at[o - 1, t, :, cols(c)],
            y_send.at[o - 1, t, c], y_recv.at[o - 1, t, c], dev(a, partners[o - 1]),
        )

    def by_distance(body):
        for d in range(A - 1, 0, -1):
            for t in (a + d, a - d):
                @pl.when((t >= 0) & (t < A))
                def _():
                    body(t)
        body(a)

    for o in range(1, B):
        line = partners[o - 1]
        for t in range(A):
            for c in range(C):
                ag_wait(line, t, c)
        project(line)
        y = jnp.dot(hid[line], wd[...], preferred_element_type=F32)
        part[line] = y.astype(BF16).reshape(A, rows, D)

        def send(t):
            for c in range(C):
                y_copy(t, c, o).start()

        by_distance(send)

    own[...] = jnp.dot(hid[b], wd[...], preferred_element_type=F32).reshape(A, rows, D)

    def right_copy(t, c):
        return rcopy(
            sbuf.at[t, :, cols(c)], rbuf.at[t, :, cols(c)],
            c_send.at[t, c], r_recv.at[t, c], dev(a + 1, b),
        )

    def left_copy(t, c):
        return rcopy(
            sbuf.at[t, :, cols(c)], lbuf.at[t, :, cols(c)],
            c_send.at[t, c], l_recv.at[t, c], dev(a - 1, b),
        )

    def add_y(t, c):
        total = own[t, :, cols(c)]
        for o in range(1, B):
            y_copy(t, c, o).wait_recv()
            total += ybuf[o - 1, t, :, cols(c)].astype(F32)
        own[t, :, cols(c)] = total

    def add_left(t, c):
        @pl.when(has_left)
        def _():
            right_copy(t, c).wait_recv()
            own[t, :, cols(c)] += rbuf[t, :, cols(c)].astype(F32)

    def add_right(t, c):
        @pl.when(has_right)
        def _():
            left_copy(t, c).wait_recv()
            own[t, :, cols(c)] += lbuf[t, :, cols(c)].astype(F32)

    for d in range(A - 1, 0, -1):
        for c in range(C):
            @pl.when(a + d < A)
            def _():
                t = a + d
                add_y(t, c)
                add_left(t, c)
                sbuf[t, :, cols(c)] = own[t, :, cols(c)].astype(BF16)
                right_copy(t, c).start()

            @pl.when(a - d >= 0)
            def _():
                t = a - d
                add_y(t, c)
                add_right(t, c)
                sbuf[t, :, cols(c)] = own[t, :, cols(c)].astype(BF16)
                left_copy(t, c).start()

    for c in range(C):
        add_y(a, c)
        add_left(a, c)
        add_right(a, c)
        out[:, cols(c)] = own[a, :, cols(c)].astype(out.dtype)

    for t in range(A):
        for c in range(C):
            @pl.when(has_right & (t <= a))
            def _():
                ag_right(t, c, tokens).wait_send()

            @pl.when(has_left & (t >= a))
            def _():
                ag_left(t, c, tokens).wait_send()

            for o in range(1, B):
                ag_across(t, c, o, tokens).wait_send()
                y_copy(t, c, o).wait_send()

            @pl.when(t != a)
            def _():
                right_copy(t, c).wait_send()


def on_device(n, tokens, gate_weight, up_weight, down_weight, format_codes, scale_exponents):
    A, B = lines_of(n)
    C = 4
    rows, D = tokens.shape
    hidden = gate_weight.shape[0]
    vmem = pl.BlockSpec(memory_space=pltpu.VMEM)
    hbm = pl.BlockSpec(memory_space=pl.ANY)
    dma = pltpu.SemaphoreType.DMA
    return pl.pallas_call(
        functools.partial(kernel, A, B, C),
        out_shape=jax.ShapeDtypeStruct((rows, D), BF16),
        in_specs=[hbm] * 6,
        out_specs=vmem,
        scratch_shapes=[
            pltpu.VMEM((B, A, rows, D), BF16),
            pltpu.VMEM((hidden, D), BF16),
            pltpu.VMEM((hidden, D), BF16),
            pltpu.VMEM((hidden, D), BF16),
            pltpu.VMEM(format_codes.shape, jnp.int32),
            pltpu.VMEM(scale_exponents.shape, jnp.int32),
            pltpu.VMEM((B, A * rows, hidden), BF16),
            pltpu.VMEM((B, A, rows, D), BF16),
            pltpu.VMEM((A, rows, D), F32),
            pltpu.VMEM((A, rows, D), BF16),
            pltpu.VMEM((B - 1, A, rows, D), BF16),
            pltpu.VMEM((A, rows, D), BF16),
            pltpu.VMEM((A, rows, D), BF16),
            dma((5,)),
            dma(()),
            dma((B, A, C)),
            dma((A, C)),
            dma((A, C)),
            dma((B - 1, A, C)),
            dma((B - 1, A, C)),
            dma((B - 1, A, C)),
            dma((A, C)),
            dma((A, C)),
            dma((A, C)),
        ],
        compiler_params=pltpu.CompilerParams(
            collective_id=0, has_side_effects=True, vmem_limit_bytes=60 * 2**20
        ),
    )(tokens, gate_weight, up_weight, down_weight, format_codes, scale_exponents)


def solution(mesh):
    return jax.shard_map(
        functools.partial(on_device, mesh.shape["tensor"]),
        mesh=mesh,
        in_specs=(
            P(("groups", "dp", "tensor"), None),
            P("tensor", None),
            P("tensor", None),
            P("tensor", None),
            P(None, "tensor"),
            P(None, "tensor"),
        ),
        out_specs=P(("groups", "dp", "tensor"), None),
        check_vma=False,
    )
```

```python
import functools
import math

import jax
import jax.numpy as jnp
from jax import lax
from jax.experimental import pallas as pl
from jax.experimental.pallas import tpu as pltpu
from jax.sharding import PartitionSpec as P

MESH = pl.DeviceIdType.MESH
F32 = jnp.float32
BF16 = jnp.bfloat16


def lines_of(n):
    inner = math.isqrt(n)
    while n % inner:
        inner -= 1
    return n // inner, inner


def kernel(
    A, B, C, tokens, gate_w, up_w, down_w, codes_in, exps_in, out,
    tok, wg, wu, wd, codes, exps, hid, part, own, sbuf, ybuf, rbuf, lbuf,
    w_sem, tok_sem, ag_recv, ag_r, ag_l, ag_y, y_send, y_recv, c_send, r_recv, l_recv,
):
    me = lax.axis_index("tensor")
    a, b = me // B, lax.rem(me, B)
    rows, D = tokens.shape
    width = D // C
    has_left, has_right = a > 0, a < A - 1

    def cols(c):
        return pl.ds(c * width, width)

    def dev(za, yb):
        return {"tensor": za * B + yb}

    def rcopy(src, dst, ssem, rsem, device):
        return pltpu.make_async_remote_copy(
            src_ref=src, dst_ref=dst, send_sem=ssem, recv_sem=rsem,
            device_id=device, device_id_type=MESH,
        )

    barrier = pltpu.get_barrier_semaphore()
    partners = [lax.rem(b + o, B) for o in range(1, B)]
    for p in partners:
        pl.semaphore_signal(barrier, inc=1, device_id=dev(a, p), device_id_type=MESH)

    @pl.when(has_left)
    def _():
        pl.semaphore_signal(barrier, inc=1, device_id=dev(a - 1, b), device_id_type=MESH)

    @pl.when(has_right)
    def _():
        pl.semaphore_signal(barrier, inc=1, device_id=dev(a + 1, b), device_id_type=MESH)

    own_tokens = pltpu.make_async_copy(tokens, tok.at[b, a], tok_sem)
    own_tokens.start()
    loads = [
        pltpu.make_async_copy(src, dst, w_sem.at[i])
        for i, (src, dst) in enumerate(
            ((codes_in, codes), (exps_in, exps), (gate_w, wg), (up_w, wu), (down_w, wd))
        )
    ]
    for load in loads:
        load.start()

    peers = B - 1 + jnp.minimum(a, 1) + jnp.minimum(A - 1 - a, 1)
    pl.semaphore_wait(barrier, peers)

    def ag_copy(t, c, src, ssem, device):
        return rcopy(
            src.at[:, cols(c)], tok.at[b, t, :, cols(c)], ssem, ag_recv.at[b, t, c], device
        )

    def ag_right(t, c, src):
        return ag_copy(t, c, src, ag_r.at[t, c], dev(a + 1, b))

    def ag_left(t, c, src):
        return ag_copy(t, c, src, ag_l.at[t, c], dev(a - 1, b))

    def ag_across(t, c, o, src):
        return ag_copy(t, c, src, ag_y.at[o - 1, t, c], dev(a, partners[o - 1]))

    def ag_wait(line, t, c):
        block = tok.at[line, t, :, cols(c)]
        rcopy(block, block, ag_r.at[t, c], ag_recv.at[line, t, c], dev(a, partners[0])).wait_recv()

    for c in range(C):
        @pl.when(has_right)
        def _():
            ag_right(a, c, tokens).start()

        @pl.when(has_left)
        def _():
            ag_left(a, c, tokens).start()

        for o in range(1, B):
            ag_across(a, c, o, tokens).start()

    dims = (((1,), (1,)), ((), ()))

    def project(line, c):
        x = tok[line, :, :, cols(c)].reshape(A * rows, width)
        return (
            lax.dot_general(x, wg[:, cols(c)], dims, preferred_element_type=F32),
            lax.dot_general(x, wu[:, cols(c)], dims, preferred_element_type=F32),
        )

    def finish(line, gate, up):
        offset = exps[...] - (7 + 8 * codes[...])
        factor = jnp.where(offset < 0, 0.5, jnp.where(offset > 0, 2.0, 1.0)).astype(F32)
        gate, up = gate * factor[0:1, :], up * factor[1:2, :]
        h = (jax.nn.gelu(gate, approximate=True) * up).astype(BF16)
        hid[line] = (h.astype(F32) * factor[2:3, :]).astype(BF16)

    gate = up = 0.0
    for s in range(1, A):
        t_left, t_right = a - s, a + s
        if s == A - 1:
            own_tokens.wait()
            for load in loads[:4]:
                load.wait()
        for c in range(C):
            @pl.when(t_left >= 0)
            def _():
                ag_wait(b, t_left, c)

                @pl.when(has_right)
                def _():
                    ag_right(t_left, c, tok.at[b, t_left]).start()

                for o in range(1, B):
                    ag_across(t_left, c, o, tok.at[b, t_left]).start()

            @pl.when(t_right < A)
            def _():
                ag_wait(b, t_right, c)

                @pl.when(has_left)
                def _():
                    ag_left(t_right, c, tok.at[b, t_right]).start()

                for o in range(1, B):
                    ag_across(t_right, c, o, tok.at[b, t_right]).start()

            if s == A - 1:
                gate_c, up_c = project(b, c)
                gate += gate_c
                up += up_c

    finish(b, gate, up)

    def y_copy(t, c, o):
        return rcopy(
            part.at[partners[o - 1], t, :, cols(c)], ybuf.at[o - 1, t, :, cols(c)],
            y_send.at[o - 1, t, c], y_recv.at[o - 1, t, c], dev(a, partners[o - 1]),
        )

    def by_distance(body):
        for d in range(A - 1, 0, -1):
            for t in (a + d, a - d):
                @pl.when((t >= 0) & (t < A) & (t != far))
                def _():
                    body(t)
        pl.when(a != far)(lambda: body(a))

    far = jnp.where(2 * a < A, A - 1, 0)

    for o in range(1, B):
        line = partners[o - 1]
        gate = up = 0.0
        for c in range(C):
            for t in range(A):
                ag_wait(line, t, c)
            gate_c, up_c = project(line, c)
            gate += gate_c
            up += up_c
        finish(line, gate, up)
        if o == 1:
            loads[4].wait()
        for c in range(C):
            y = jnp.dot(hid[line], wd[:, cols(c)], preferred_element_type=F32)
            part[line, :, :, cols(c)] = y.astype(BF16).reshape(A, rows, width)
            y_copy(far, c, o).start()

        def send(t):
            for c in range(C):
                y_copy(t, c, o).start()

        by_distance(send)

    own[...] = jnp.dot(hid[b], wd[...], preferred_element_type=F32).reshape(A, rows, D)

    def right_copy(t, c):
        return rcopy(
            sbuf.at[t, :, cols(c)], rbuf.at[t, :, cols(c)],
            c_send.at[t, c], r_recv.at[t, c], dev(a + 1, b),
        )

    def left_copy(t, c):
        return rcopy(
            sbuf.at[t, :, cols(c)], lbuf.at[t, :, cols(c)],
            c_send.at[t, c], l_recv.at[t, c], dev(a - 1, b),
        )

    def add_y(t, c):
        total = own[t, :, cols(c)]
        for o in range(1, B):
            y_copy(t, c, o).wait_recv()
            total += ybuf[o - 1, t, :, cols(c)].astype(F32)
        own[t, :, cols(c)] = total

    def add_left(t, c):
        @pl.when(has_left)
        def _():
            right_copy(t, c).wait_recv()
            own[t, :, cols(c)] += rbuf[t, :, cols(c)].astype(F32)

    def add_right(t, c):
        @pl.when(has_right)
        def _():
            left_copy(t, c).wait_recv()
            own[t, :, cols(c)] += lbuf[t, :, cols(c)].astype(F32)

    for d in range(A - 1, 0, -1):
        for c in range(C):
            @pl.when(a + d < A)
            def _():
                t = a + d
                add_y(t, c)
                add_left(t, c)
                sbuf[t, :, cols(c)] = own[t, :, cols(c)].astype(BF16)
                right_copy(t, c).start()

            @pl.when(a - d >= 0)
            def _():
                t = a - d
                add_y(t, c)
                add_right(t, c)
                sbuf[t, :, cols(c)] = own[t, :, cols(c)].astype(BF16)
                left_copy(t, c).start()

    for c in range(C):
        add_y(a, c)
        add_left(a, c)
        add_right(a, c)
        out[:, cols(c)] = own[a, :, cols(c)].astype(out.dtype)

    for t in range(A):
        for c in range(C):
            @pl.when(has_right & (t <= a))
            def _():
                ag_right(t, c, tokens).wait_send()

            @pl.when(has_left & (t >= a))
            def _():
                ag_left(t, c, tokens).wait_send()

            for o in range(1, B):
                ag_across(t, c, o, tokens).wait_send()
                y_copy(t, c, o).wait_send()

            @pl.when(t != a)
            def _():
                right_copy(t, c).wait_send()


def on_device(n, tokens, gate_weight, up_weight, down_weight, format_codes, scale_exponents):
    A, B = lines_of(n)
    C = 4 if n <= 8 else 2
    rows, D = tokens.shape
    hidden = gate_weight.shape[0]
    vmem = pl.BlockSpec(memory_space=pltpu.VMEM)
    hbm = pl.BlockSpec(memory_space=pl.ANY)
    dma = pltpu.SemaphoreType.DMA
    return pl.pallas_call(
        functools.partial(kernel, A, B, C),
        out_shape=pltpu.VMEM((rows, D), BF16),
        in_specs=[hbm] * 6,
        out_specs=vmem,
        scratch_shapes=[
            pltpu.VMEM((B, A, rows, D), BF16),
            pltpu.VMEM((hidden, D), BF16),
            pltpu.VMEM((hidden, D), BF16),
            pltpu.VMEM((hidden, D), BF16),
            pltpu.VMEM(format_codes.shape, jnp.int32),
            pltpu.VMEM(scale_exponents.shape, jnp.int32),
            pltpu.VMEM((B, A * rows, hidden), BF16),
            pltpu.VMEM((B, A, rows, D), BF16),
            pltpu.VMEM((A, rows, D), F32),
            pltpu.VMEM((A, rows, D), BF16),
            pltpu.VMEM((B - 1, A, rows, D), BF16),
            pltpu.VMEM((A, rows, D), BF16),
            pltpu.VMEM((A, rows, D), BF16),
            dma((5,)),
            dma(()),
            dma((B, A, C)),
            dma((A, C)),
            dma((A, C)),
            dma((B - 1, A, C)),
            dma((B - 1, A, C)),
            dma((B - 1, A, C)),
            dma((A, C)),
            dma((A, C)),
            dma((A, C)),
        ],
        compiler_params=pltpu.CompilerParams(
            collective_id=0, has_side_effects=True, vmem_limit_bytes=60 * 2**20
        ),
    )(tokens, gate_weight, up_weight, down_weight, format_codes, scale_exponents)


def solution(mesh):
    return jax.shard_map(
        functools.partial(on_device, mesh.shape["tensor"]),
        mesh=mesh,
        in_specs=(
            P(("groups", "dp", "tensor"), None),
            P("tensor", None),
            P("tensor", None),
            P("tensor", None),
            P(None, "tensor"),
            P(None, "tensor"),
        ),
        out_specs=P(("groups", "dp", "tensor"), None),
        check_vma=False,
    )
```

```python
import functools
import math

import jax
import jax.numpy as jnp
from jax import lax
from jax.experimental import pallas as pl
from jax.experimental.pallas import tpu as pltpu
from jax.sharding import PartitionSpec as P

MESH = pl.DeviceIdType.MESH
F32 = jnp.float32
BF16 = jnp.bfloat16


def lines_of(n):
    inner = math.isqrt(n)
    while n % inner:
        inner -= 1
    return n // inner, inner


def kernel(
    A, B, C, tokens, gate_w, up_w, down_w, codes_in, exps_in, out,
    tok, wg, wu, wd, codes, exps, hid, part, own, sbuf, ybuf, rbuf, lbuf,
    w_sem, tok_sem, ag_recv, ag_r, ag_l, ag_y, y_send, y_recv, c_send, r_recv, l_recv,
):
    me = lax.axis_index("tensor")
    a, b = me // B, lax.rem(me, B)
    rows, D = tokens.shape
    width = D // C
    has_left, has_right = a > 0, a < A - 1

    def cols(c):
        return pl.ds(c * width, width)

    def dev(za, yb):
        return {"tensor": za * B + yb}

    def rcopy(src, dst, ssem, rsem, device):
        return pltpu.make_async_remote_copy(
            src_ref=src, dst_ref=dst, send_sem=ssem, recv_sem=rsem,
            device_id=device, device_id_type=MESH,
        )

    barrier = pltpu.get_barrier_semaphore()
    partners = [lax.rem(b + o, B) for o in range(1, B)]
    for p in partners:
        pl.semaphore_signal(barrier, inc=1, device_id=dev(a, p), device_id_type=MESH)

    @pl.when(has_left)
    def _():
        pl.semaphore_signal(barrier, inc=1, device_id=dev(a - 1, b), device_id_type=MESH)

    @pl.when(has_right)
    def _():
        pl.semaphore_signal(barrier, inc=1, device_id=dev(a + 1, b), device_id_type=MESH)

    own_tokens = pltpu.make_async_copy(tokens, tok.at[b, a], tok_sem)
    own_tokens.start()
    loads = [
        pltpu.make_async_copy(src, dst, w_sem.at[i])
        for i, (src, dst) in enumerate(
            ((codes_in, codes), (exps_in, exps), (gate_w, wg), (up_w, wu), (down_w, wd))
        )
    ]
    peers = B - 1 + jnp.minimum(a, 1) + jnp.minimum(A - 1 - a, 1)
    pl.semaphore_wait(barrier, peers)

    def ag_copy(t, c, src, ssem, device):
        return rcopy(
            src.at[:, cols(c)], tok.at[b, t, :, cols(c)], ssem, ag_recv.at[b, t, c], device
        )

    def ag_right(t, c, src):
        return ag_copy(t, c, src, ag_r.at[t, c], dev(a + 1, b))

    def ag_left(t, c, src):
        return ag_copy(t, c, src, ag_l.at[t, c], dev(a - 1, b))

    def ag_across(t, c, o, src):
        return ag_copy(t, c, src, ag_y.at[o - 1, t, c], dev(a, partners[o - 1]))

    def ag_wait(line, t, c):
        block = tok.at[line, t, :, cols(c)]
        rcopy(block, block, ag_r.at[t, c], ag_recv.at[line, t, c], dev(a, partners[0])).wait_recv()

    for c in range(C):
        @pl.when(has_right)
        def _():
            ag_right(a, c, tokens).start()

        @pl.when(has_left)
        def _():
            ag_left(a, c, tokens).start()

        for o in range(1, B):
            ag_across(a, c, o, tokens).start()

    for load in loads:
        load.start()

    dims = (((1,), (1,)), ((), ()))

    def project(line, c):
        x = tok[line, :, :, cols(c)].reshape(A * rows, width)
        return (
            lax.dot_general(x, wg[:, cols(c)], dims, preferred_element_type=F32),
            lax.dot_general(x, wu[:, cols(c)], dims, preferred_element_type=F32),
        )

    def finish(line, gate, up):
        offset = exps[...] - (7 + 8 * codes[...])
        factor = jnp.where(offset < 0, 0.5, jnp.where(offset > 0, 2.0, 1.0)).astype(F32)
        gate, up = gate * factor[0:1, :], up * factor[1:2, :]
        h = (jax.nn.gelu(gate, approximate=True) * up).astype(BF16)
        hid[line] = (h.astype(F32) * factor[2:3, :]).astype(BF16)

    gate = up = 0.0
    for s in range(1, A):
        t_left, t_right = a - s, a + s
        if s == A - 1:
            own_tokens.wait()
            for load in loads[:4]:
                load.wait()
        for c in range(C):
            @pl.when(t_left >= 0)
            def _():
                ag_wait(b, t_left, c)

                @pl.when(has_right)
                def _():
                    ag_right(t_left, c, tok.at[b, t_left]).start()

                for o in range(1, B):
                    ag_across(t_left, c, o, tok.at[b, t_left]).start()

            @pl.when(t_right < A)
            def _():
                ag_wait(b, t_right, c)

                @pl.when(has_left)
                def _():
                    ag_left(t_right, c, tok.at[b, t_right]).start()

                for o in range(1, B):
                    ag_across(t_right, c, o, tok.at[b, t_right]).start()

            if s == A - 1:
                gate_c, up_c = project(b, c)
                gate += gate_c
                up += up_c

    finish(b, gate, up)

    def y_copy(t, c, o):
        return rcopy(
            part.at[partners[o - 1], t, :, cols(c)], ybuf.at[o - 1, t, :, cols(c)],
            y_send.at[o - 1, t, c], y_recv.at[o - 1, t, c], dev(a, partners[o - 1]),
        )

    def by_distance(body):
        for d in range(A - 1, 0, -1):
            for t in (a + d, a - d):
                @pl.when((t >= 0) & (t < A) & (t != far))
                def _():
                    body(t)
        pl.when(a != far)(lambda: body(a))

    far = jnp.where(2 * a < A, A - 1, 0)

    for o in range(1, B):
        line = partners[o - 1]
        gate = up = 0.0
        for c in range(C):
            for t in range(A):
                ag_wait(line, t, c)
            gate_c, up_c = project(line, c)
            gate += gate_c
            up += up_c
        finish(line, gate, up)
        if o == 1:
            loads[4].wait()
        for c in range(C):
            y = jnp.dot(hid[line], wd[:, cols(c)], preferred_element_type=F32)
            part[line, :, :, cols(c)] = y.astype(BF16).reshape(A, rows, width)
            y_copy(far, c, o).start()

        def send(t):
            for c in range(C):
                y_copy(t, c, o).start()

        by_distance(send)

    own[...] = jnp.dot(hid[b], wd[...], preferred_element_type=F32).reshape(A, rows, D)

    def right_copy(t, c):
        return rcopy(
            sbuf.at[t, :, cols(c)], rbuf.at[t, :, cols(c)],
            c_send.at[t, c], r_recv.at[t, c], dev(a + 1, b),
        )

    def left_copy(t, c):
        return rcopy(
            sbuf.at[t, :, cols(c)], lbuf.at[t, :, cols(c)],
            c_send.at[t, c], l_recv.at[t, c], dev(a - 1, b),
        )

    def add_y(t, c):
        total = own[t, :, cols(c)]
        for o in range(1, B):
            y_copy(t, c, o).wait_recv()
            total += ybuf[o - 1, t, :, cols(c)].astype(F32)
        own[t, :, cols(c)] = total

    def add_left(t, c):
        @pl.when(has_left)
        def _():
            right_copy(t, c).wait_recv()
            own[t, :, cols(c)] += rbuf[t, :, cols(c)].astype(F32)

    def add_right(t, c):
        @pl.when(has_right)
        def _():
            left_copy(t, c).wait_recv()
            own[t, :, cols(c)] += lbuf[t, :, cols(c)].astype(F32)

    for d in range(A - 1, 0, -1):
        for c in range(C):
            @pl.when(a + d < A)
            def _():
                t = a + d
                add_y(t, c)
                add_left(t, c)
                sbuf[t, :, cols(c)] = own[t, :, cols(c)].astype(BF16)
                right_copy(t, c).start()

            @pl.when(a - d >= 0)
            def _():
                t = a - d
                add_y(t, c)
                add_right(t, c)
                sbuf[t, :, cols(c)] = own[t, :, cols(c)].astype(BF16)
                left_copy(t, c).start()

    for c in range(C):
        add_y(a, c)
        add_left(a, c)
        add_right(a, c)
        out[:, cols(c)] = own[a, :, cols(c)].astype(out.dtype)

    for t in range(A):
        for c in range(C):
            @pl.when(has_right & (t <= a))
            def _():
                ag_right(t, c, tokens).wait_send()

            @pl.when(has_left & (t >= a))
            def _():
                ag_left(t, c, tokens).wait_send()

            for o in range(1, B):
                ag_across(t, c, o, tokens).wait_send()
                y_copy(t, c, o).wait_send()

            @pl.when(t != a)
            def _():
                right_copy(t, c).wait_send()


def on_device(n, tokens, gate_weight, up_weight, down_weight, format_codes, scale_exponents):
    A, B = lines_of(n)
    C = 4 if n <= 8 else 2
    rows, D = tokens.shape
    hidden = gate_weight.shape[0]
    vmem = pl.BlockSpec(memory_space=pltpu.VMEM)
    hbm = pl.BlockSpec(memory_space=pl.ANY)
    dma = pltpu.SemaphoreType.DMA
    return pl.pallas_call(
        functools.partial(kernel, A, B, C),
        out_shape=pltpu.VMEM((rows, D), BF16),
        in_specs=[hbm] * 6,
        out_specs=vmem,
        scratch_shapes=[
            pltpu.VMEM((B, A, rows, D), BF16),
            pltpu.VMEM((hidden, D), BF16),
            pltpu.VMEM((hidden, D), BF16),
            pltpu.VMEM((hidden, D), BF16),
            pltpu.VMEM(format_codes.shape, jnp.int32),
            pltpu.VMEM(scale_exponents.shape, jnp.int32),
            pltpu.VMEM((B, A * rows, hidden), BF16),
            pltpu.VMEM((B, A, rows, D), BF16),
            pltpu.VMEM((A, rows, D), F32),
            pltpu.VMEM((A, rows, D), BF16),
            pltpu.VMEM((B - 1, A, rows, D), BF16),
            pltpu.VMEM((A, rows, D), BF16),
            pltpu.VMEM((A, rows, D), BF16),
            dma((5,)),
            dma(()),
            dma((B, A, C)),
            dma((A, C)),
            dma((A, C)),
            dma((B - 1, A, C)),
            dma((B - 1, A, C)),
            dma((B - 1, A, C)),
            dma((A, C)),
            dma((A, C)),
            dma((A, C)),
        ],
        compiler_params=pltpu.CompilerParams(
            collective_id=0, has_side_effects=True, vmem_limit_bytes=60 * 2**20
        ),
    )(tokens, gate_weight, up_weight, down_weight, format_codes, scale_exponents)


def solution(mesh):
    return jax.shard_map(
        functools.partial(on_device, mesh.shape["tensor"]),
        mesh=mesh,
        in_specs=(
            P(("groups", "dp", "tensor"), None),
            P("tensor", None),
            P("tensor", None),
            P("tensor", None),
            P(None, "tensor"),
            P(None, "tensor"),
        ),
        out_specs=P(("groups", "dp", "tensor"), None),
        check_vma=False,
    )
```
